32 devices in a mesh: view: 2 (over y), tile: 16 (over z, x, core).
Axes of the slice: x: 2, y: 2, z: 4, core: 2. Of those that a mesh axis runs over, the one named last changes fastest.
Arguments:
- estimate: float32 [384, 512, 128], P('tile', 'view'), may hold values from 0.5 to 2
- raw_tiles: bfloat16 [4, 384, 512, 128], P('view', 'tile'), may hold values from 0.19921875 to 3
- psf_taps: float32 [4, 3, 17], replicated, may hold values from 0.05 to 1
- view_offsets: int32 [4, 3], replicated, may hold values from -4 to 4, as said below
- depth_range: int32 [4, 16, 2], P(None, 'tile'), may hold values from 0 to 128, as said below
Outputs:
- new_estimate: float32 [384, 512, 128], P('tile', 'view')
The draws below stay inside these ranges and needn't reach their ends.
Inputs may be any that keep to these rules, and one draw needn't show every extreme that they name: `view_offsets`: some view's offset along the first dimension is 4 and some view's offset along the second dimension is -4. `depth_range`: entry 0 is the first valid depth plane of a view in a raw tile and entry 1 is one past its last; entry 0 < 64 < entry 1.
All inputs are finite; a program needn't handle non-finite values.
Results may differ from the reference program's by a relative error of at most 0.0003.
Values may be sent and summed in bfloat16 or wider, within the bound.
A program may use at most 192 MiB of HBM per device.

```python
import math
import jax
import jax.numpy as jnp
from jax import lax

BX = 24
NY = 512
NZ = 128
TAPS = 17
MAXOFF = 4
VIEWS = 4
TILES = 16
NX = 384


def draw_view_offsets(key, part):
    shift_key, pick_key = jax.random.split(key, 2)
    drawn = jax.random.randint(shift_key, (VIEWS, 3), -MAXOFF, MAXOFF + 1)
    picked = jax.random.randint(pick_key, (2,), 0, VIEWS)
    view_index = jnp.arange(VIEWS)[:, None]
    axis_index = jnp.arange(3)[None, :]
    drawn = jnp.where((view_index == picked[0]) & (axis_index == 0), MAXOFF, drawn)
    drawn = jnp.where((view_index == picked[1]) & (axis_index == 1), -MAXOFF, drawn)
    return drawn.astype(jnp.int32)


def draw_depth_range(key, part):
    first_key, last_key, pick_key = jax.random.split(key, 3)
    first_plane = jax.random.randint(first_key, (VIEWS, TILES), 0, NZ // 2)
    last_plane = jax.random.randint(last_key, (VIEWS, TILES), NZ // 2 + 1, NZ + 1)
    picked = jax.random.randint(pick_key, (2,), 0, VIEWS * TILES)
    flat_index = jnp.arange(VIEWS * TILES).reshape(VIEWS, TILES)
    first_plane = jnp.where(flat_index == picked[0], 0, first_plane)
    last_plane = jnp.where(flat_index == picked[1], NZ, last_plane)
    return jnp.stack([first_plane, last_plane], axis=-1).astype(jnp.int32)


def shard_levels(stream_key, shape, cuts, low, high):
    factor_of = 1.0
    for axis_at, blocks in cuts:
        draws = jax.random.uniform(jax.random.fold_in(jax.random.fold_in(stream_key, 6), axis_at), (blocks,), jnp.float32, low / len(cuts), high / len(cuts))
        factor_of = factor_of * jnp.repeat(jnp.exp(draws), shape[axis_at] // blocks).reshape((-1,) + (1,) * (len(shape) - 1 - axis_at))
    return factor_of


def setup_inputs(seed: int = 0) -> dict:
    arg_keys = jax.random.split(jax.random.key(seed), 6)
    estimate = jnp.clip(0.5 + 1.5 * jax.random.uniform(arg_keys[0], (NX, NY, NZ), jnp.float32) ** shard_levels(arg_keys[0], (NX, NY, NZ), ((0, 16), (1, 2)), -0.2, 0.2), 0.5, 2.0)
    raw_tiles = jnp.clip(0.19921875 + 2.8007812 * jax.random.uniform(arg_keys[1], (VIEWS, NX, NY, NZ), jnp.float32) ** shard_levels(arg_keys[1], (VIEWS, NX, NY, NZ), ((0, 2), (1, 16)), -0.2, 0.2), 0.19921875, 3.0).astype(jnp.bfloat16)
    psf_taps = jnp.clip(jnp.exp(jax.random.uniform(arg_keys[2], (VIEWS, 3, TAPS), jnp.float32, math.log(0.05), math.log(1.0))), 0.05, 1.0)
    view_offsets = draw_view_offsets(jax.random.fold_in(arg_keys[5], 71), 0)
    depth_range = draw_depth_range(jax.random.fold_in(arg_keys[5], 71), 0)
    return {"estimate": estimate, "raw_tiles": raw_tiles, "psf_taps": psf_taps, "view_offsets": view_offsets, "depth_range": depth_range}


BACKGROUND = 0.1
FLOOR = 0.5


def shifted_sum(volume, kernel, offset, dimension, direction):
    margin = TAPS // 2 + MAXOFF
    length = volume.shape[dimension]
    widths = [(margin, margin) if dimension_index == dimension else (0, 0) for dimension_index in range(3)]
    padded = jnp.pad(volume, widths)
    summed = jnp.zeros_like(volume)
    for tap_index in range(TAPS):
        begin_at = (margin + direction * (offset + tap_index - TAPS // 2)).astype(jnp.int32)
        window = lax.dynamic_slice_in_dim(padded, begin_at, length, dimension)
        summed = summed + kernel[tap_index] * window
    return summed


def blur_all(volume, kernels, offsets, direction):
    for dimension in range(3):
        volume = shifted_sum(volume, kernels[dimension], offsets[dimension], dimension, direction)
    return volume


def reference(estimate, raw_tiles, psf_taps, view_offsets, depth_range):
    kernels = psf_taps / jnp.sum(psf_taps, axis=2, keepdims=True)
    tile_of_plane = jnp.arange(NX) // BX
    depth_index = jnp.arange(NZ)

    def add_view(view_number, running):
        correction, weight = running
        view_kernels = kernels[view_number]
        offsets = view_offsets[view_number]
        first_plane = depth_range[view_number, :, 0][tile_of_plane]
        last_plane = depth_range[view_number, :, 1][tile_of_plane]
        inside = ((depth_index[None, :] >= first_plane[:, None]) & (depth_index[None, :] < last_plane[:, None])).astype(jnp.float32)
        coverage = jnp.broadcast_to(inside[:, None, :], estimate.shape)
        predicted = blur_all(estimate, view_kernels, offsets, 1)
        quotient = coverage * raw_tiles[view_number].astype(jnp.float32) / (predicted + BACKGROUND)
        correction = correction + blur_all(quotient, view_kernels, offsets, -1)
        weight = weight + blur_all(coverage, view_kernels, offsets, -1)
        return correction, weight

    zeroed = jnp.zeros(estimate.shape, jnp.float32)
    correction, weight = lax.fori_loop(0, VIEWS, add_view, (zeroed, zeroed))
    return estimate * correction / jnp.maximum(weight, FLOOR)
```

```python
import functools

import jax
import jax.numpy as jnp
from jax import lax
from jax.experimental import pallas as pl
from jax.experimental.pallas import tpu as pltpu
from jax.sharding import PartitionSpec as P

MAXOFF = 4
BACKGROUND = 0.1
FLOOR = 0.5
EST_MID = 1.25
QUO_MID = 1.1875
SUB = 8
ROWS = 16
PLANES = 4
F32 = jnp.float32
BF16 = jnp.bfloat16
VMEM_LIMIT = 48 * 1024 * 1024


def tap_lookup(kernel, number):
    total = jnp.zeros(number.shape, kernel.dtype)
    for tap in range(kernel.shape[1]):
        value = kernel[:, tap].reshape((-1,) + (1,) * (number.ndim - 1))
        total = jnp.where(number == tap, value, total)
    return total


def rows_forward_kernel(est_ref, matrix_ref, out_ref):
    views, planes, rows, depth = out_ref.shape
    for pair in range(0, planes, 2):
        data = jnp.concatenate([est_ref[pair], est_ref[pair + 1]], axis=1)
        done = jnp.dot(matrix_ref[...], data, preferred_element_type=F32)
        for view in range(views):
            part = done[view * rows : (view + 1) * rows].astype(out_ref.dtype)
            out_ref[view, pair] = part[:, :depth]
            out_ref[view, pair + 1] = part[:, depth:]


def rows_forward(est, matrix, views):
    count, rows_in, depth = est.shape
    rows = matrix.shape[0] // views
    return pl.pallas_call(
        rows_forward_kernel,
        grid=(count // PLANES,),
        in_specs=[
            pl.BlockSpec((PLANES, rows_in, depth), lambda i: (i, 0, 0)),
            pl.BlockSpec(matrix.shape, lambda i: (0, 0)),
        ],
        out_specs=pl.BlockSpec((views, PLANES, rows, depth), lambda i: (0, i, 0, 0)),
        out_shape=jax.ShapeDtypeStruct((views, count, rows, depth), BF16),
        compiler_params=pltpu.CompilerParams(vmem_limit_bytes=VMEM_LIMIT),
        cost_estimate=pl.CostEstimate(
            flops=2 * count * depth * rows_in * views * rows,
            bytes_accessed=2 * (est.size + views * count * rows * depth),
            transcendentals=0,
        ),
    )(est, matrix)


def view_kernel(
    scalar_ref,
    inner_ref,
    outer_ref,
    raw_ref,
    plane_ref,
    plane_t_ref,
    depth_ref,
    depth_t_ref,
    ones_x_ref,
    ones_yz_ref,
    cover_ref,
    scale_ref,
    out_ref,
    ext_ref,
):
    block, _, depth = raw_ref.shape
    halo = outer_ref.shape[0] // 2
    window = plane_ref.shape[1] // SUB
    start = scalar_ref[0]
    ext_ref[:halo] = outer_ref[:halo]
    ext_ref[halo : halo + block] = inner_ref[...]
    ext_ref[halo + block :] = outer_ref[halo:]
    source = ext_ref[pl.ds(start, window)].astype(F32)
    halves = [
        source[:, lo : lo + SUB].reshape(window * SUB, depth) for lo in range(0, ROWS, SUB)
    ]
    data = jnp.concatenate(halves, axis=1).astype(BF16)
    planes = jnp.dot(plane_ref[...], data, preferred_element_type=F32)
    stacked = jnp.concatenate([planes[:, :depth], planes[:, depth:]], axis=0).astype(BF16)
    blurred = jnp.dot(stacked, depth_ref[...], preferred_element_type=F32)
    blurred = blurred.reshape(2, block, SUB, depth)
    raw = raw_ref[...].astype(F32)
    scale = scale_ref[...]
    cover = cover_ref[...] * scale
    ones_x = ones_x_ref[...]
    quotients = []
    for half in range(2):
        ones_yz = ones_yz_ref[half * SUB : (half + 1) * SUB]
        predicted = blurred[half] * scale + ones_x * ones_yz
        ratio = raw[:, half * SUB : (half + 1) * SUB] / (predicted + BACKGROUND)
        quotients.append((cover * (ratio - QUO_MID)).reshape(block * SUB, depth))
    quotient = jnp.concatenate(quotients, axis=0).astype(BF16)
    back = jnp.dot(quotient, depth_t_ref[...], preferred_element_type=F32)
    size = block * SUB
    back = jnp.concatenate([back[:size], back[size:]], axis=1).astype(BF16)
    spread = jnp.dot(plane_t_ref[...], back, preferred_element_type=F32)
    spread = [
        spread[:, lo : lo + depth].reshape(window, SUB, depth) for lo in (0, depth)
    ]
    out_ref[...] = jnp.zeros_like(out_ref)
    out_ref[pl.ds(start, window)] = jnp.concatenate(spread, axis=1).astype(out_ref.dtype)


def view_pass(view, slot, base, start, inner, outer, raw, tables):
    _, block, rows, depth = inner.shape
    halo2 = outer.shape[1]
    plane, plane_t, depth_m, depth_mt, ones_x, ones_yz, cover, scale = tables
    scalars = jnp.stack([start, base]).astype(jnp.int32)

    def table(array):
        zeros = (0,) * (array.ndim - 1)
        return pl.BlockSpec((None,) + array.shape[1:], lambda g, s: (view,) + zeros)

    rows_block = pl.BlockSpec((None, block, ROWS, depth), lambda g, s: (view, 0, g, 0))
    outer_block = pl.BlockSpec((None, halo2, ROWS, depth), lambda g, s: (view, 0, g, 0))
    return pl.pallas_call(
        view_kernel,
        grid_spec=pltpu.PrefetchScalarGridSpec(
            num_scalar_prefetch=1,
            grid=(rows // ROWS,),
            in_specs=[
                rows_block,
                outer_block,
                pl.BlockSpec((None, block, ROWS, depth), lambda g, s: (slot, 0, s[1] + g, 0)),
                table(plane),
                table(plane_t),
                table(depth_m),
                table(depth_mt),
                table(ones_x),
                pl.BlockSpec((None, ROWS, depth), lambda g, s: (view, g, 0)),
                table(cover),
                table(scale),
            ],
            out_specs=pl.BlockSpec((block + halo2, ROWS, depth), lambda g, s: (0, g, 0)),
            scratch_shapes=[pltpu.VMEM((block + halo2, ROWS, depth), BF16)],
        ),
        out_shape=jax.ShapeDtypeStruct((block + halo2, rows, depth), BF16),
        compiler_params=pltpu.CompilerParams(vmem_limit_bytes=VMEM_LIMIT),
        cost_estimate=pl.CostEstimate(
            flops=2 * (rows // ROWS) * 2_000 * 256 * 256,
            bytes_accessed=2 * rows * depth * (5 * block),
            transcendentals=block * rows * depth,
        ),
    )(
        scalars,
        inner,
        outer,
        raw,
        plane,
        plane_t,
        depth_m,
        depth_mt,
        ones_x,
        ones_yz,
        cover,
        scale,
    )


def rows_back_kernel(*refs):
    *part_refs, matrix_ref, out_ref = refs
    planes, _, depth = out_ref.shape
    for pair in range(0, planes, 2):
        data = jnp.concatenate(
            [jnp.concatenate([ref[pair], ref[pair + 1]], axis=1) for ref in part_refs], axis=0
        )
        done = jnp.dot(matrix_ref[...], data, preferred_element_type=F32).astype(out_ref.dtype)
        out_ref[pair] = done[:, :depth]
        out_ref[pair + 1] = done[:, depth:]


def rows_back(parts, matrix, blocks, place, dtype):
    _, rows, depth = parts[0].shape
    rows_out = matrix.shape[0]
    return pl.pallas_call(
        rows_back_kernel,
        grid=(blocks,),
        in_specs=[pl.BlockSpec((PLANES, rows, depth), lambda i: (place(i), 0, 0)) for _ in parts]
        + [pl.BlockSpec(matrix.shape, lambda i: (0, 0))],
        out_specs=pl.BlockSpec((PLANES, rows_out, depth), lambda i: (i, 0, 0)),
        out_shape=jax.ShapeDtypeStruct((blocks * PLANES, rows_out, depth), dtype),
        compiler_params=pltpu.CompilerParams(vmem_limit_bytes=VMEM_LIMIT),
        cost_estimate=pl.CostEstimate(
            flops=2 * blocks * PLANES * depth * matrix.size,
            bytes_accessed=2 * blocks * PLANES * depth * (len(parts) * rows + 2 * rows_out),
            transcendentals=0,
        ),
    )(*parts, matrix)


def on_device(estimate, raw_tiles, psf_taps, view_offsets, depth_range):
    block, half_rows, depth = estimate.shape
    slots = raw_tiles.shape[0]
    views, _, taps = psf_taps.shape
    half = taps // 2
    halo = half + MAXOFF
    tiles = lax.axis_size("tile")
    tile = lax.axis_index("tile")
    place = lax.axis_index("view")
    planes_all = block * tiles
    rows_all = half_rows * lax.axis_size("view")
    swap = [(0, 1), (1, 0)]
    up = [(i, i + 1) for i in range(tiles - 1)]
    down = [(i + 1, i) for i in range(tiles - 1)]
    quo_rows = half_rows + ROWS
    est_extra = 2 * ROWS
    iota = functools.partial(lax.broadcasted_iota, jnp.int32)

    centred = (estimate - EST_MID).astype(BF16)
    edge = lax.dynamic_slice_in_dim(centred, (1 - place) * (half_rows - est_extra), est_extra, 1)
    inner_est = jnp.concatenate([centred, lax.ppermute(edge, "view", swap)], axis=1)
    outer_est = jnp.concatenate(
        [
            lax.ppermute(inner_est[block - halo :], "tile", up),
            lax.ppermute(inner_est[:halo], "tile", down),
        ],
        axis=0,
    )

    other_start = (1 - place) * (half_rows - ROWS)
    arrived = []
    for slot in range(slots):
        piece = lax.dynamic_slice_in_dim(raw_tiles[slot], other_start, quo_rows, 1)
        arrived.append(lax.ppermute(piece, "view", swap)[None])

    def own_first(array):
        return jnp.where(place == 0, array, jnp.roll(array, slots, axis=0))

    raw_taps = own_first(psf_taps)
    offsets = own_first(view_offsets)
    kernels = raw_taps / jnp.sum(raw_taps, axis=2, keepdims=True)
    rounded = kernels.astype(BF16).astype(F32)
    scale = 1.0 / jnp.prod(jnp.sum(rounded, axis=2), axis=1)
    limits = jnp.stack(
        [
            lax.ppermute(depth_range, "tile", up),
            depth_range,
            lax.ppermute(depth_range, "tile", down),
        ]
    )
    limits = own_first(limits[:, :, 0].transpose(1, 0, 2))
    depth_index = jnp.arange(depth)
    cover3 = (
        (depth_index >= limits[:, :, :1]) & (depth_index < limits[:, :, 1:])
    ).astype(F32)

    ox, oy, oz = (offsets[:, dim] for dim in range(3))
    window = block + taps - 1

    shape = (views, block * SUB, window * SUB)
    row, column = iota(shape, 1), iota(shape, 2)
    step = jnp.where(row % SUB == column % SUB, column // SUB - row // SUB, -1)
    plane_m = tap_lookup(rounded[:, 0], step).astype(BF16)
    plane_mt = plane_m.transpose(0, 2, 1)

    shape = (views, depth, depth)
    depth_m = tap_lookup(
        rounded[:, 2], iota(shape, 1) - iota(shape, 2) - oz[:, None, None] + half
    ).astype(BF16)
    depth_mt = depth_m.transpose(0, 2, 1)

    quo_first = place * (half_rows - ROWS)
    shape = (views, quo_rows, half_rows + est_extra)
    position = iota(shape, 2)
    from_row = jnp.where(
        position < half_rows,
        place * half_rows + position,
        (1 - place) * half_rows + place * (half_rows - est_extra) + position - half_rows,
    )
    to_row = quo_first + iota(shape, 1)
    rows_m = tap_lookup(rounded[:, 1], from_row - to_row - oy[:, None, None] + half)
    rows_m = rows_m.astype(BF16).reshape(views * quo_rows, half_rows + est_extra)

    shape = (views, half_rows, quo_rows)
    to_row = place * half_rows + iota(shape, 1)
    from_row = quo_first + iota(shape, 2)
    rows_mt = tap_lookup(rounded[:, 1], to_row - from_row - oy[:, None, None] + half)
    rows_mt = rows_mt.astype(BF16).transpose(1, 0, 2).reshape(half_rows, views * quo_rows)

    tap = jnp.arange(taps)

    def inside_sum(kernel, index, count):
        inside = (index >= 0) & (index < count)
        return jnp.sum(jnp.where(inside, kernel[:, None, :], 0.0), axis=2)

    def reached(first, count, offset, direction):
        base = first + jnp.arange(count)
        return base[None, :, None] + direction * (offset[:, None, None] + tap - half)

    ones_x = inside_sum(kernels[:, 0], reached(tile * block, block, ox, 1), planes_all)
    ones_y = inside_sum(kernels[:, 1], reached(quo_first, quo_rows, oy, 1), rows_all)
    ones_z = inside_sum(kernels[:, 2], reached(0, depth, oz, 1), depth)
    ones_yz = EST_MID * ones_y[:, :, None] * ones_z[:, None, :]
    ones_x = jnp.broadcast_to(ones_x[:, :, None, None], (views, block, SUB, depth))
    cover = jnp.broadcast_to(cover3[:, 1][:, None, :], (views, SUB, depth))
    scales = jnp.broadcast_to(scale[:, None, None], (views, SUB, depth))
    tables = (plane_m, plane_mt, depth_m, depth_mt, ones_x, ones_yz, cover, scales)

    taken = jnp.einsum(
        "wkj,wij->wki",
        cover3,
        tap_lookup(
            kernels[:, 2],
            iota((views, depth, depth), 1) - iota((views, depth, depth), 2)
            - oz[:, None, None]
            + half,
        ),
        precision=lax.Precision.HIGHEST,
    )
    from_plane = reached(0, block, ox, -1)
    table_xz = 0.0
    for side in range(3):
        low = (side - 1) * block
        share = inside_sum(kernels[:, 0], from_plane - low, block)
        table_xz = table_xz + share[:, :, None] * taken[:, side][:, None, :]
    back_y = inside_sum(
        kernels[:, 1], reached(place * half_rows, half_rows, oy, -1), rows_all
    )

    inner = rows_forward(inner_est, rows_m, views)
    outer = rows_forward(outer_est, rows_m, views)
    starts = ox + (halo - half)
    parts = []
    for view in range(views):
        mine = view < slots
        parts.append(
            view_pass(
                view,
                view if mine else 0,
                place * ((half_rows - ROWS) // ROWS) if mine else jnp.int32(0),
                starts[view],
                inner,
                outer,
                raw_tiles if mine else arrived[view - slots],
                tables,
            )
        )

    side = halo // PLANES
    middle = block // PLANES
    edges = rows_back(
        parts, rows_mt, 2 * side, lambda i: jnp.where(i < side, i, i + middle), BF16
    )
    kept = rows_back(parts, rows_mt, middle, lambda i: i + side, F32)
    low = lax.ppermute(edges[halo:], "tile", up)
    high = lax.ppermute(edges[:halo], "tile", down)
    low = jnp.pad(low, ((0, block - halo), (0, 0), (0, 0)))
    high = jnp.pad(high, ((block - halo, 0), (0, 0), (0, 0)))
    weight = sum(
        table_xz[view][:, None, :] * back_y[view][None, :, None] for view in range(views)
    )
    correction = kept + low.astype(F32) + high.astype(F32) + QUO_MID * weight
    return estimate * correction / jnp.maximum(weight, FLOOR)


def solution(mesh):
    return jax.shard_map(
        on_device,
        mesh=mesh,
        in_specs=(
            P("tile", "view", None),
            P("view", "tile", None, None),
            P(),
            P(),
            P(None, "tile", None),
        ),
        out_specs=P("tile", "view", None),
        check_vma=False,
    )
```

```python
import functools

import jax
import jax.numpy as jnp
from jax import lax
from jax.experimental import pallas as pl
from jax.experimental.pallas import tpu as pltpu
from jax.sharding import PartitionSpec as P

MAXOFF = 4
BACKGROUND = 0.1
FLOOR = 0.5
EST_MID = 1.25
QUO_MID = 1.1875
SUB = 8
ROWS = 16
PLANES = 4
F32 = jnp.float32
BF16 = jnp.bfloat16
VMEM_LIMIT = 48 * 1024 * 1024


def banded(taps, number):
    total = jnp.zeros(number.shape, F32)
    for index, tap in enumerate(taps):
        total = jnp.where(number == index, tap, total)
    return total


def inside_sum(taps, first, step, low, high):
    total = jnp.zeros(first.shape, F32)
    for index, tap in enumerate(taps):
        at = first + step * index
        total = total + jnp.where((at >= low) & (at < high), tap, 0.0)
    return total


def tables_kernel(
    exact_ref,
    rounded_ref,
    scale_in_ref,
    offset_ref,
    range_ref,
    position_ref,
    rows_ref,
    rows_t_ref,
    plane_ref,
    plane_t_ref,
    depth_ref,
    depth_t_ref,
    ones_x_ref,
    ones_yz_ref,
    cover_ref,
    scale_ref,
    *,
    slots,
    tiles,
    rows_all,
):
    views, _, taps = exact_ref.shape
    half = taps // 2
    half_rows = rows_t_ref.shape[0]
    quo_rows = ones_yz_ref.shape[1]
    est_rows = rows_ref.shape[1]
    est_extra = est_rows - half_rows
    block, depth = ones_x_ref.shape[1], ones_x_ref.shape[3]
    place, tile = position_ref[0], position_ref[1]
    quo_first = place * (half_rows - ROWS)
    order = [lax.rem(place * slots + w, views) for w in range(views)]
    rounded = [
        [[rounded_ref[w, d, a] for a in range(taps)] for d in range(3)] for w in order
    ]
    exact = [[[exact_ref[w, d, a] for a in range(taps)] for d in range(3)] for w in order]
    offsets = [[offset_ref[w, d] for d in range(3)] for w in order]

    def iota(shape, dim):
        return lax.broadcasted_iota(jnp.int32, shape, dim)

    for w in range(views):
        ox, oy, oz = offsets[w]

        def plane_rows(i, carry, w=w):
            shape = (ROWS, plane_ref.shape[2])
            row, column = iota(shape, 0) + i * ROWS, iota(shape, 1)
            step = jnp.where(
                (row & (SUB - 1)) == (column & (SUB - 1)), (column >> 3) - (row >> 3), -1
            )
            at = pl.ds(pl.multiple_of(i * ROWS, ROWS), ROWS)
            plane_ref[w, at] = banded(rounded[w][0], step).astype(BF16)
            return carry

        lax.fori_loop(0, plane_ref.shape[1] // ROWS, plane_rows, 0)

        def plane_t_rows(i, carry, w=w):
            shape = (ROWS, plane_t_ref.shape[2])
            row, column = iota(shape, 0) + i * ROWS, iota(shape, 1)
            step = jnp.where(
                (row & (SUB - 1)) == (column & (SUB - 1)), (row >> 3) - (column >> 3), -1
            )
            at = pl.ds(pl.multiple_of(i * ROWS, ROWS), ROWS)
            plane_t_ref[w, at] = banded(rounded[w][0], step).astype(BF16)
            return carry

        lax.fori_loop(0, plane_t_ref.shape[1] // ROWS, plane_t_rows, 0)

        def depth_rows(i, carry, w=w, oz=oz):
            shape = (ROWS, depth)
            away = iota(shape, 0) + i * ROWS - iota(shape, 1)
            at = pl.ds(pl.multiple_of(i * ROWS, ROWS), ROWS)
            depth_ref[w, at] = banded(rounded[w][2], away - oz + half).astype(BF16)
            depth_t_ref[w, at] = banded(rounded[w][2], half - oz - away).astype(BF16)
            return carry

        lax.fori_loop(0, depth // ROWS, depth_rows, 0)

        def forward_rows(i, carry, w=w, oy=oy):
            shape = (ROWS, est_rows)
            position = iota(shape, 1)
            from_row = jnp.where(
                position < half_rows,
                place * half_rows + position,
                (1 - place) * half_rows
                + place * (half_rows - est_extra)
                + position
                - half_rows,
            )
            to_row = quo_first + i * ROWS + iota(shape, 0)
            value = banded(rounded[w][1], from_row - to_row - oy + half).astype(BF16)
            at = pl.multiple_of(w * quo_rows + i * ROWS, ROWS)
            rows_ref[pl.ds(at, ROWS)] = value
            return carry

        lax.fori_loop(0, quo_rows // ROWS, forward_rows, 0)

        shape = (block, SUB, depth)
        first = tile * block + iota(shape, 0) + ox - half
        ones_x_ref[w] = inside_sum(exact[w][0], first, 1, 0, tiles * block)
        first = quo_first + iota((quo_rows, depth), 0) + oy - half
        ones_y = inside_sum(exact[w][1], first, 1, 0, rows_all)
        shape = (SUB, depth)
        z = iota(shape, 1)
        ones_z = inside_sum(exact[w][2], z + oz - half, 1, 0, depth)
        ones_yz_ref[w] = EST_MID * ones_y * ones_z[:1]
        low, high = range_ref[order[w], 0, 0], range_ref[order[w], 0, 1]
        cover_ref[w] = jnp.where((z >= low) & (z < high), 1.0, 0.0)
        scale_ref[w] = jnp.full(shape, scale_in_ref[order[w]], F32)

    def back_rows(i, carry):
        shape = (ROWS, quo_rows)
        away = place * half_rows + i * ROWS + iota(shape, 0) - quo_first - iota(shape, 1)
        value = [banded(rounded[w][1], away - offsets[w][1] + half) for w in range(views)]
        at = pl.ds(pl.multiple_of(i * ROWS, ROWS), ROWS)
        rows_t_ref[at] = jnp.concatenate(value, axis=1).astype(BF16)
        return carry

    lax.fori_loop(0, half_rows // ROWS, back_rows, 0)


def weight_tables_kernel(
    exact_ref, offset_ref, below_ref, range_ref, above_ref, position_ref, xz_ref, y_ref, *, rows_all
):
    views, _, taps = exact_ref.shape
    half = taps // 2
    block, depth = xz_ref.shape[1:]
    half_rows = y_ref.shape[1]
    place = position_ref[0]

    def iota(shape, dim):
        return lax.broadcasted_iota(jnp.int32, shape, dim)

    for w in range(views):
        ox, oy, oz = (offset_ref[w, d] for d in range(3))
        exact = [[exact_ref[w, d, a] for a in range(taps)] for d in range(3)]
        plane = iota((block, depth), 0) - ox + half
        z = iota((SUB, depth), 1) - oz + half
        total = jnp.zeros((block, depth), F32)
        for side, limit in enumerate((below_ref, range_ref, above_ref)):
            low = (side - 1) * block
            share = inside_sum(exact[0], plane, -1, low, low + block)
            taken = inside_sum(exact[2], z, -1, limit[w, 0, 0], limit[w, 0, 1])
            total = total + share * taken[:1]
        xz_ref[w] = total
        first = place * half_rows + iota((half_rows, depth), 0) - oy + half
        y_ref[w] = inside_sum(exact[1], first, -1, 0, rows_all)


def finish_kernel(est_ref, kept_ref, low_ref, high_ref, xz_ref, y_ref, out_ref, *, sides):
    planes = est_ref.shape[0]
    views = y_ref.shape[0]
    step = pl.program_id(0)
    is_low = jnp.where(step < sides, 1.0, 0.0)
    for plane in range(planes):
        at = pl.ds(step * planes + plane, 1)
        weight = sum(y_ref[w] * xz_ref[w, at] for w in range(views))
        edge = low_ref[plane].astype(F32) * is_low + high_ref[plane].astype(F32) * (1.0 - is_low)
        correction = kept_ref[plane] + edge + QUO_MID * weight
        out_ref[plane] = est_ref[plane] * correction / jnp.maximum(weight, FLOOR)


def rows_forward_kernel(est_ref, matrix_ref, out_ref):
    views, groups, planes, _, depth = out_ref.shape
    rows = groups * ROWS
    for pair in range(0, planes, 2):
        data = jnp.concatenate([est_ref[pair], est_ref[pair + 1]], axis=1)
        done = jnp.dot(matrix_ref[...], data, preferred_element_type=F32).astype(BF16)
        for view in range(views):
            part = done[view * rows : (view + 1) * rows]
            out_ref[view, :, pair] = part[:, :depth].reshape(groups, ROWS, depth)
            out_ref[view, :, pair + 1] = part[:, depth:].reshape(groups, ROWS, depth)


def rows_forward(est, matrix, views):
    count, rows_in, depth = est.shape
    rows = matrix.shape[0] // views
    groups = rows // ROWS
    return pl.pallas_call(
        rows_forward_kernel,
        grid=(count // PLANES,),
        in_specs=[
            pl.BlockSpec((PLANES, rows_in, depth), lambda i: (i, 0, 0)),
            pl.BlockSpec(matrix.shape, lambda i: (0, 0)),
        ],
        out_specs=pl.BlockSpec(
            (views, groups, PLANES, ROWS, depth), lambda i: (0, 0, i, 0, 0)
        ),
        out_shape=jax.ShapeDtypeStruct((views, groups, count, ROWS, depth), BF16),
        compiler_params=pltpu.CompilerParams(vmem_limit_bytes=VMEM_LIMIT),
        cost_estimate=pl.CostEstimate(
            flops=2 * count * depth * rows_in * views * rows,
            bytes_accessed=2 * (est.size + views * count * rows * depth),
            transcendentals=0,
        ),
    )(est, matrix)


def view_kernel(
    scalar_ref,
    inner_ref,
    outer_ref,
    raw_ref,
    plane_ref,
    plane_t_ref,
    depth_ref,
    depth_t_ref,
    ones_x_ref,
    ones_yz_ref,
    cover_ref,
    scale_ref,
    out_ref,
    ext_ref,
):
    slots, block, _, depth = raw_ref.shape
    halo = outer_ref.shape[1] // 2
    window = plane_ref.shape[2] // SUB
    size = block * SUB
    every = range(slots)
    starts = [scalar_ref[1 + w] for w in every]
    ext_ref[:, :halo] = outer_ref[:, :halo]
    ext_ref[:, halo : halo + block] = inner_ref[...]
    ext_ref[:, halo + block :] = outer_ref[:, halo:]
    stacked = []
    for w in every:
        source = ext_ref[w, pl.ds(starts[w], window)].astype(F32)
        halves = [
            source[:, lo : lo + SUB].reshape(window * SUB, depth) for lo in range(0, ROWS, SUB)
        ]
        data = jnp.concatenate(halves, axis=1).astype(BF16)
        planes = jnp.dot(plane_ref[w], data, preferred_element_type=F32)
        stacked.append(
            jnp.concatenate([planes[:, :depth], planes[:, depth:]], axis=0).astype(BF16)
        )
    blurred = [
        jnp.dot(stacked[w], depth_ref[w], preferred_element_type=F32).reshape(
            2, block, SUB, depth
        )
        for w in every
    ]
    quotient = []
    for w in every:
        raw = raw_ref[w].astype(F32)
        scale = scale_ref[w]
        cover = cover_ref[w] * scale
        halves = []
        for half in range(2):
            ones_yz = ones_yz_ref[w, half * SUB : (half + 1) * SUB]
            predicted = blurred[w][half] * scale + ones_x_ref[w] * ones_yz
            ratio = raw[:, half * SUB : (half + 1) * SUB] / (predicted + BACKGROUND)
            halves.append((cover * (ratio - QUO_MID)).reshape(size, depth))
        quotient.append(jnp.concatenate(halves, axis=0).astype(BF16))
    back = [
        jnp.dot(quotient[w], depth_t_ref[w], preferred_element_type=F32) for w in every
    ]
    out_ref[...] = jnp.zeros_like(out_ref)
    for w in every:
        wide = jnp.concatenate([back[w][:size], back[w][size:]], axis=1).astype(BF16)
        spread = jnp.dot(plane_t_ref[w], wide, preferred_element_type=F32)
        spread = [
            spread[:, lo : lo + depth].reshape(window, SUB, depth) for lo in (0, depth)
        ]
        out_ref[w, pl.ds(starts[w], window)] = jnp.concatenate(spread, axis=1).astype(
            out_ref.dtype
        )


def view_pass(pair, slots, first, groups, base, starts, inner, outer, raw, tables):
    _, _, block, _, depth = inner.shape
    halo2 = outer.shape[2]
    plane, plane_t, depth_m, depth_mt, ones_x, ones_yz, cover, scale = tables
    scalars = jnp.concatenate([base[None], starts]).astype(jnp.int32)

    def table(array):
        zeros = (0,) * (array.ndim - 1)
        return pl.BlockSpec((slots,) + array.shape[1:], lambda g, s: (pair,) + zeros)

    def grouped(planes):
        return pl.BlockSpec(
            (slots, None, planes, ROWS, depth), lambda g, s: (pair, first + g, 0, 0, 0)
        )

    return pl.pallas_call(
        view_kernel,
        grid_spec=pltpu.PrefetchScalarGridSpec(
            num_scalar_prefetch=1,
            grid=(groups,),
            in_specs=[
                grouped(block),
                grouped(halo2),
                pl.BlockSpec((slots, block, ROWS, depth), lambda g, s: (0, 0, s[0] + g, 0)),
                table(plane),
                table(plane_t),
                table(depth_m),
                table(depth_mt),
                table(ones_x),
                pl.BlockSpec((slots, ROWS, depth), lambda g, s: (pair, first + g, 0)),
                table(cover),
                table(scale),
            ],
            out_specs=pl.BlockSpec(
                (slots, None, block + halo2, ROWS, depth), lambda g, s: (0, g, 0, 0, 0)
            ),
            scratch_shapes=[pltpu.VMEM((slots, block + halo2, ROWS, depth), BF16)],
        ),
        out_shape=jax.ShapeDtypeStruct((slots, groups, block + halo2, ROWS, depth), BF16),
        compiler_params=pltpu.CompilerParams(vmem_limit_bytes=VMEM_LIMIT),
        cost_estimate=pl.CostEstimate(
            flops=2 * slots * groups * 3_000 * 256 * 256,
            bytes_accessed=2 * slots * groups * ROWS * depth * (5 * block),
            transcendentals=slots * block * groups * ROWS * depth,
        ),
    )(scalars, inner, outer, raw, plane, plane_t, depth_m, depth_mt, ones_x, ones_yz, cover, scale)


def rows_back_kernel(*refs):
    *part_refs, matrix_ref, out_ref = refs
    own_ref, *other_refs = part_refs
    planes, _, depth = out_ref.shape

    def rows_of(ref, slot, plane):
        return ref[slot, :, plane].reshape(ref.shape[1] * ROWS, depth)

    for pair in range(0, planes, 2):
        pieces = []
        for refs_of in ((own_ref,), other_refs):
            for slot in range(own_ref.shape[0]):
                for ref in refs_of:
                    pieces.append(
                        jnp.concatenate(
                            [rows_of(ref, slot, pair), rows_of(ref, slot, pair + 1)], axis=1
                        )
                    )
        data = jnp.concatenate(pieces, axis=0)
        done = jnp.dot(matrix_ref[...], data, preferred_element_type=F32).astype(out_ref.dtype)
        out_ref[pair] = done[:, :depth]
        out_ref[pair + 1] = done[:, depth:]


def rows_back(parts, matrix, blocks, place, dtype):
    depth = parts[0].shape[-1]
    rows_out = matrix.shape[0]

    def planes_of(part):
        return pl.BlockSpec(
            part.shape[:2] + (PLANES, ROWS, depth), lambda i: (0, 0, place(i), 0, 0)
        )

    return pl.pallas_call(
        rows_back_kernel,
        grid=(blocks,),
        in_specs=[planes_of(part) for part in parts]
        + [pl.BlockSpec(matrix.shape, lambda i: (0, 0))],
        out_specs=pl.BlockSpec((PLANES, rows_out, depth), lambda i: (i, 0, 0)),
        out_shape=jax.ShapeDtypeStruct((blocks * PLANES, rows_out, depth), dtype),
        compiler_params=pltpu.CompilerParams(vmem_limit_bytes=VMEM_LIMIT),
        cost_estimate=pl.CostEstimate(
            flops=2 * blocks * PLANES * depth * matrix.size,
            bytes_accessed=2 * blocks * PLANES * depth * (matrix.shape[1] + 2 * rows_out),
            transcendentals=0,
        ),
    )(*parts, matrix)


def on_device(estimate, raw_tiles, psf_taps, view_offsets, depth_range):
    block, half_rows, depth = estimate.shape
    slots = raw_tiles.shape[0]
    views, _, taps = psf_taps.shape
    half = taps // 2
    halo = half + MAXOFF
    tiles = lax.axis_size("tile")
    place = lax.axis_index("view")
    rows_all = half_rows * lax.axis_size("view")
    swap = [(0, 1), (1, 0)]
    up = [(i, i + 1) for i in range(tiles - 1)]
    down = [(i + 1, i) for i in range(tiles - 1)]
    quo_rows = half_rows + ROWS
    groups = quo_rows // ROWS
    est_extra = 2 * ROWS
    window = block + taps - 1

    start = (1 - place) * (half_rows - est_extra)
    edge = lax.dynamic_slice_in_dim(estimate, start, est_extra, 1)
    edge = (edge - EST_MID).astype(BF16)
    centred = (estimate - EST_MID).astype(BF16)
    inner_est = jnp.concatenate([centred, lax.ppermute(edge, "view", swap)], axis=1)
    outer_est = jnp.concatenate(
        [
            lax.ppermute(inner_est[block - halo :], "tile", up),
            lax.ppermute(inner_est[:halo], "tile", down),
        ],
        axis=0,
    )

    other_start = (1 - place) * (half_rows - ROWS)
    cuts = [0, (groups + 1) // 2, groups]
    arrived = []
    for low, high in zip(cuts, cuts[1:]):
        piece = lax.dynamic_slice_in_dim(
            raw_tiles, other_start + low * ROWS, (high - low) * ROWS, 2
        )
        arrived.append(lax.ppermute(piece, "view", swap))

    kernels = psf_taps / jnp.sum(psf_taps, axis=2, keepdims=True)
    rounded = lax.reduce_precision(kernels, 8, 7)
    scale = 1.0 / jnp.prod(jnp.sum(rounded, axis=2), axis=1)
    position = jnp.stack([place, lax.axis_index("tile")]).astype(jnp.int32)

    smem = pl.BlockSpec(memory_space=pltpu.SMEM)
    vmem = pl.BlockSpec(memory_space=pltpu.VMEM)
    shapes = [
        ((views * quo_rows, half_rows + est_extra), BF16),
        ((half_rows, views * quo_rows), BF16),
        ((views, block * SUB, window * SUB), BF16),
        ((views, window * SUB, block * SUB), BF16),
        ((views, depth, depth), BF16),
        ((views, depth, depth), BF16),
        ((views, block, SUB, depth), F32),
        ((views, quo_rows, depth), F32),
        ((views, SUB, depth), F32),
        ((views, SUB, depth), F32),
    ]
    rows_m, rows_mt, *tables = pl.pallas_call(
        functools.partial(tables_kernel, slots=slots, tiles=tiles, rows_all=rows_all),
        in_specs=[smem] * 6,
        out_specs=[vmem] * len(shapes),
        out_shape=[jax.ShapeDtypeStruct(*shape) for shape in shapes],
        compiler_params=pltpu.CompilerParams(vmem_limit_bytes=VMEM_LIMIT),
        cost_estimate=pl.CostEstimate(flops=0, bytes_accessed=30_000_000, transcendentals=0),
    )(kernels, rounded, scale, view_offsets, depth_range, position)

    below = lax.ppermute(depth_range, "tile", up)
    above = lax.ppermute(depth_range, "tile", down)
    table_xz, table_y = pl.pallas_call(
        functools.partial(weight_tables_kernel, rows_all=rows_all),
        in_specs=[smem] * 6,
        out_specs=[vmem] * 2,
        out_shape=[
            jax.ShapeDtypeStruct((views, block, depth), F32),
            jax.ShapeDtypeStruct((views, half_rows, depth), F32),
        ],
        compiler_params=pltpu.CompilerParams(vmem_limit_bytes=VMEM_LIMIT),
        cost_estimate=pl.CostEstimate(flops=0, bytes_accessed=8_000_000, transcendentals=0),
    )(kernels, view_offsets, below, depth_range, above, position)

    inner = rows_forward(inner_est, rows_m, views)
    outer = rows_forward(outer_est, rows_m, views)
    own_first = lax.rem(place * slots + jnp.arange(views), views)
    starts = view_offsets[own_first, 0] + (halo - half)
    base = place * ((half_rows - ROWS) // ROWS)
    zero = jnp.zeros((), jnp.int32)
    parts = [
        view_pass(0, slots, 0, groups, base, starts[:slots], inner, outer, raw_tiles, tables)
    ]
    for low, high, piece in zip(cuts, cuts[1:], arrived):
        parts.append(
            view_pass(
                1, slots, low, high - low, zero, starts[slots:], inner, outer, piece, tables
            )
        )

    side = halo // PLANES
    middle = block // PLANES
    edges = rows_back(
        parts, rows_mt, 2 * side, lambda i: jnp.where(i < side, i, i + middle), BF16
    )
    kept = rows_back(parts, rows_mt, middle, lambda i: i + side, F32)
    low = lax.ppermute(edges[halo:], "tile", up)
    high = lax.ppermute(edges[:halo], "tile", down)
    sides = halo // PLANES
    whole = (PLANES, half_rows, depth)
    return pl.pallas_call(
        functools.partial(finish_kernel, sides=sides),
        grid=(middle,),
        in_specs=[
            pl.BlockSpec(whole, lambda i: (i, 0, 0)),
            pl.BlockSpec(whole, lambda i: (i, 0, 0)),
            pl.BlockSpec(whole, lambda i: (jnp.minimum(i, sides - 1), 0, 0)),
            pl.BlockSpec(whole, lambda i: (jnp.maximum(i - sides, 0), 0, 0)),
            pl.BlockSpec(table_xz.shape, lambda i: (0, 0, 0)),
            pl.BlockSpec(table_y.shape, lambda i: (0, 0, 0)),
        ],
        out_specs=pl.BlockSpec(whole, lambda i: (i, 0, 0)),
        out_shape=jax.ShapeDtypeStruct(estimate.shape, F32),
        compiler_params=pltpu.CompilerParams(vmem_limit_bytes=VMEM_LIMIT),
    )(estimate, kept, low, high, table_xz, table_y)


def solution(mesh):
    return jax.shard_map(
        on_device,
        mesh=mesh,
        in_specs=(
            P("tile", "view", None),
            P("view", "tile", None, None),
            P(),
            P(),
            P(None, "tile", None),
        ),
        out_specs=P("tile", "view", None),
        check_vma=False,
    )
```

```python
import functools

import jax
import jax.numpy as jnp
from jax import lax
from jax.experimental import pallas as pl
from jax.experimental.pallas import tpu as pltpu
from jax.sharding import PartitionSpec as P

MAXOFF = 4
BACKGROUND = 0.1
FLOOR = 0.5
EST_MID = 1.25
QUO_MID = 1.1875
SUB = 8
ROWS = 16
PLANES = 4
F32 = jnp.float32
BF16 = jnp.bfloat16
VMEM_LIMIT = 48 * 1024 * 1024


def banded(taps, number):
    total = jnp.zeros(number.shape, F32)
    for index, tap in enumerate(taps):
        total = jnp.where(number == index, tap, total)
    return total


def inside_sum(taps, first, step, low, high):
    total = jnp.zeros(first.shape, F32)
    for index, tap in enumerate(taps):
        at = first + step * index
        total = total + jnp.where((at >= low) & (at < high), tap, 0.0)
    return total


def tables_kernel(
    exact_ref,
    rounded_ref,
    scale_in_ref,
    offset_ref,
    range_ref,
    position_ref,
    rows_ref,
    rows_t_ref,
    plane_ref,
    plane_t_ref,
    depth_ref,
    depth_t_ref,
    ones_x_ref,
    ones_yz_ref,
    cover_ref,
    scale_ref,
    *,
    slots,
    tiles,
    rows_all,
):
    views, _, taps = exact_ref.shape
    half = taps // 2
    half_rows = rows_t_ref.shape[0]
    quo_rows = ones_yz_ref.shape[1]
    est_rows = rows_ref.shape[1]
    est_extra = est_rows - half_rows
    block, depth = ones_x_ref.shape[1], ones_x_ref.shape[3]
    place, tile = position_ref[0], position_ref[1]
    quo_first = place * (half_rows - ROWS)
    order = [lax.rem(place * slots + w, views) for w in range(views)]
    rounded = [
        [[rounded_ref[w, d, a] for a in range(taps)] for d in range(3)] for w in order
    ]
    exact = [[[exact_ref[w, d, a] for a in range(taps)] for d in range(3)] for w in order]
    offsets = [[offset_ref[w, d] for d in range(3)] for w in order]

    def iota(shape, dim):
        return lax.broadcasted_iota(jnp.int32, shape, dim)

    for w in range(views):
        ox, oy, oz = offsets[w]

        def plane_rows(i, carry, w=w):
            shape = (ROWS, plane_ref.shape[2])
            row, column = iota(shape, 0) + i * ROWS, iota(shape, 1)
            step = jnp.where(
                (row & (SUB - 1)) == (column & (SUB - 1)), (column >> 3) - (row >> 3), -1
            )
            at = pl.ds(pl.multiple_of(i * ROWS, ROWS), ROWS)
            plane_ref[w, at] = banded(rounded[w][0], step).astype(BF16)
            return carry

        lax.fori_loop(0, plane_ref.shape[1] // ROWS, plane_rows, 0)

        def plane_t_rows(i, carry, w=w):
            shape = (ROWS, plane_t_ref.shape[2])
            row, column = iota(shape, 0) + i * ROWS, iota(shape, 1)
            step = jnp.where(
                (row & (SUB - 1)) == (column & (SUB - 1)), (row >> 3) - (column >> 3), -1
            )
            at = pl.ds(pl.multiple_of(i * ROWS, ROWS), ROWS)
            plane_t_ref[w, at] = banded(rounded[w][0], step).astype(BF16)
            return carry

        lax.fori_loop(0, plane_t_ref.shape[1] // ROWS, plane_t_rows, 0)

        def depth_rows(i, carry, w=w, oz=oz):
            shape = (ROWS, depth)
            away = iota(shape, 0) + i * ROWS - iota(shape, 1)
            at = pl.ds(pl.multiple_of(i * ROWS, ROWS), ROWS)
            depth_ref[w, at] = banded(rounded[w][2], away - oz + half).astype(BF16)
            depth_t_ref[w, at] = banded(rounded[w][2], half - oz - away).astype(BF16)
            return carry

        lax.fori_loop(0, depth // ROWS, depth_rows, 0)

        def forward_rows(i, carry, w=w, oy=oy):
            shape = (ROWS, est_rows)
            position = iota(shape, 1)
            from_row = jnp.where(
                position < half_rows,
                place * half_rows + position,
                (1 - place) * half_rows
                + place * (half_rows - est_extra)
                + position
                - half_rows,
            )
            to_row = quo_first + i * ROWS + iota(shape, 0)
            value = banded(rounded[w][1], from_row - to_row - oy + half).astype(BF16)
            at = pl.multiple_of(w * quo_rows + i * ROWS, ROWS)
            rows_ref[pl.ds(at, ROWS)] = value
            return carry

        lax.fori_loop(0, quo_rows // ROWS, forward_rows, 0)

        shape = (block, SUB, depth)
        first = tile * block + iota(shape, 0) + ox - half
        ones_x_ref[w] = inside_sum(exact[w][0], first, 1, 0, tiles * block)
        first = quo_first + iota((quo_rows, depth), 0) + oy - half
        ones_y = inside_sum(exact[w][1], first, 1, 0, rows_all)
        shape = (SUB, depth)
        z = iota(shape, 1)
        ones_z = inside_sum(exact[w][2], z + oz - half, 1, 0, depth)
        ones_yz_ref[w] = EST_MID * ones_y * ones_z[:1]
        low, high = range_ref[order[w], 0, 0], range_ref[order[w], 0, 1]
        cover_ref[w] = jnp.where((z >= low) & (z < high), 1.0, 0.0)
        scale_ref[w] = jnp.full(shape, scale_in_ref[order[w]], F32)

    def back_rows(i, carry):
        shape = (ROWS, quo_rows)
        away = place * half_rows + i * ROWS + iota(shape, 0) - quo_first - iota(shape, 1)
        value = [banded(rounded[w][1], away - offsets[w][1] + half) for w in range(views)]
        at = pl.ds(pl.multiple_of(i * ROWS, ROWS), ROWS)
        rows_t_ref[at] = jnp.concatenate(value, axis=1).astype(BF16)
        return carry

    lax.fori_loop(0, half_rows // ROWS, back_rows, 0)


def weight_tables_kernel(
    exact_ref, offset_ref, below_ref, range_ref, above_ref, position_ref, xz_ref, y_ref, *, rows_all
):
    views, _, taps = exact_ref.shape
    half = taps // 2
    block, depth = xz_ref.shape[1:]
    half_rows = y_ref.shape[1]
    place = position_ref[0]

    def iota(shape, dim):
        return lax.broadcasted_iota(jnp.int32, shape, dim)

    for w in range(views):
        ox, oy, oz = (offset_ref[w, d] for d in range(3))
        exact = [[exact_ref[w, d, a] for a in range(taps)] for d in range(3)]
        plane = iota((block, depth), 0) - ox + half
        z = iota((SUB, depth), 1) - oz + half
        total = jnp.zeros((block, depth), F32)
        for side, limit in enumerate((below_ref, range_ref, above_ref)):
            low = (side - 1) * block
            share = inside_sum(exact[0], plane, -1, low, low + block)
            taken = inside_sum(exact[2], z, -1, limit[w, 0, 0], limit[w, 0, 1])
            total = total + share * taken[:1]
        xz_ref[w] = total
        first = place * half_rows + iota((half_rows, depth), 0) - oy + half
        y_ref[w] = inside_sum(exact[1], first, -1, 0, rows_all)


def finish_kernel(kept_ref, factor_ref, low_ref, high_ref, out_ref, *, sides):
    step = pl.program_id(0)
    is_low = jnp.where(step < sides, 1.0, 0.0)
    edge = low_ref[...].astype(F32) * is_low + high_ref[...].astype(F32) * (1.0 - is_low)
    out_ref[...] = factor_ref[...] * (kept_ref[...] + edge)


def rows_forward_kernel(est_ref, matrix_ref, out_ref):
    views, groups, planes, _, depth = out_ref.shape
    rows = groups * ROWS
    for pair in range(0, planes, 2):
        data = jnp.concatenate([est_ref[pair], est_ref[pair + 1]], axis=1)
        done = jnp.dot(matrix_ref[...], data, preferred_element_type=F32).astype(BF16)
        for view in range(views):
            part = done[view * rows : (view + 1) * rows]
            out_ref[view, :, pair] = part[:, :depth].reshape(groups, ROWS, depth)
            out_ref[view, :, pair + 1] = part[:, depth:].reshape(groups, ROWS, depth)


def rows_forward(est, matrix, views):
    count, rows_in, depth = est.shape
    rows = matrix.shape[0] // views
    groups = rows // ROWS
    return pl.pallas_call(
        rows_forward_kernel,
        grid=(count // PLANES,),
        in_specs=[
            pl.BlockSpec((PLANES, rows_in, depth), lambda i: (i, 0, 0)),
            pl.BlockSpec(matrix.shape, lambda i: (0, 0)),
        ],
        out_specs=pl.BlockSpec(
            (views, groups, PLANES, ROWS, depth), lambda i: (0, 0, i, 0, 0)
        ),
        out_shape=jax.ShapeDtypeStruct((views, groups, count, ROWS, depth), BF16),
        compiler_params=pltpu.CompilerParams(vmem_limit_bytes=VMEM_LIMIT),
        cost_estimate=pl.CostEstimate(
            flops=2 * count * depth * rows_in * views * rows,
            bytes_accessed=2 * (est.size + views * count * rows * depth),
            transcendentals=0,
        ),
    )(est, matrix)


def view_kernel(
    scalar_ref,
    inner_ref,
    outer_ref,
    raw_ref,
    plane_ref,
    plane_t_ref,
    depth_ref,
    depth_t_ref,
    ones_x_ref,
    ones_yz_ref,
    cover_ref,
    scale_ref,
    out_ref,
    ext_ref,
):
    slots, block, _, depth = raw_ref.shape
    halo = outer_ref.shape[1] // 2
    window = plane_ref.shape[2] // SUB
    size = block * SUB
    every = range(slots)
    starts = [scalar_ref[1 + w] for w in every]
    ext_ref[:, :halo] = outer_ref[:, :halo]
    ext_ref[:, halo : halo + block] = inner_ref[...]
    ext_ref[:, halo + block :] = outer_ref[:, halo:]
    stacked = []
    for w in every:
        source = ext_ref[w, pl.ds(starts[w], window)].astype(F32)
        halves = [
            source[:, lo : lo + SUB].reshape(window * SUB, depth) for lo in range(0, ROWS, SUB)
        ]
        data = jnp.concatenate(halves, axis=1).astype(BF16)
        planes = jnp.dot(plane_ref[w], data, preferred_element_type=F32)
        stacked.append(
            jnp.concatenate([planes[:, :depth], planes[:, depth:]], axis=0).astype(BF16)
        )
    blurred = [
        jnp.dot(stacked[w], depth_ref[w], preferred_element_type=F32).reshape(
            2, block, SUB, depth
        )
        for w in every
    ]
    quotient = []
    for w in every:
        raw = raw_ref[w].astype(F32)
        scale = scale_ref[w]
        cover = cover_ref[w] * scale
        halves = []
        for half in range(2):
            ones_yz = ones_yz_ref[w, half * SUB : (half + 1) * SUB]
            predicted = blurred[w][half] * scale + ones_x_ref[w] * ones_yz
            ratio = raw[:, half * SUB : (half + 1) * SUB] / (predicted + BACKGROUND)
            halves.append((cover * (ratio - QUO_MID)).reshape(size, depth))
        quotient.append(jnp.concatenate(halves, axis=0).astype(BF16))
    back = [
        jnp.dot(quotient[w], depth_t_ref[w], preferred_element_type=F32) for w in every
    ]
    out_ref[...] = jnp.zeros_like(out_ref)
    for w in every:
        wide = jnp.concatenate([back[w][:size], back[w][size:]], axis=1).astype(BF16)
        spread = jnp.dot(plane_t_ref[w], wide, preferred_element_type=F32)
        spread = [
            spread[:, lo : lo + depth].reshape(window, SUB, depth) for lo in (0, depth)
        ]
        out_ref[w, pl.ds(starts[w], window)] = jnp.concatenate(spread, axis=1).astype(
            out_ref.dtype
        )


def view_pass(pair, slots, first, groups, base, starts, inner, outer, raw, tables):
    _, _, block, _, depth = inner.shape
    halo2 = outer.shape[2]
    plane, plane_t, depth_m, depth_mt, ones_x, ones_yz, cover, scale = tables
    scalars = jnp.concatenate([base[None], starts]).astype(jnp.int32)

    def table(array):
        zeros = (0,) * (array.ndim - 1)
        return pl.BlockSpec((slots,) + array.shape[1:], lambda g, s: (pair,) + zeros)

    def grouped(planes):
        return pl.BlockSpec(
            (slots, None, planes, ROWS, depth), lambda g, s: (pair, first + g, 0, 0, 0)
        )

    return pl.pallas_call(
        view_kernel,
        grid_spec=pltpu.PrefetchScalarGridSpec(
            num_scalar_prefetch=1,
            grid=(groups,),
            in_specs=[
                grouped(block),
                grouped(halo2),
                pl.BlockSpec((slots, block, ROWS, depth), lambda g, s: (0, 0, s[0] + g, 0)),
                table(plane),
                table(plane_t),
                table(depth_m),
                table(depth_mt),
                table(ones_x),
                pl.BlockSpec((slots, ROWS, depth), lambda g, s: (pair, first + g, 0)),
                table(cover),
                table(scale),
            ],
            out_specs=pl.BlockSpec(
                (slots, None, block + halo2, ROWS, depth), lambda g, s: (0, g, 0, 0, 0)
            ),
            scratch_shapes=[pltpu.VMEM((slots, block + halo2, ROWS, depth), BF16)],
        ),
        out_shape=jax.ShapeDtypeStruct((slots, groups, block + halo2, ROWS, depth), BF16),
        compiler_params=pltpu.CompilerParams(vmem_limit_bytes=VMEM_LIMIT),
        cost_estimate=pl.CostEstimate(
            flops=2 * slots * groups * 3_000 * 256 * 256,
            bytes_accessed=2 * slots * groups * ROWS * depth * (5 * block),
            transcendentals=slots * block * groups * ROWS * depth,
        ),
    )(scalars, inner, outer, raw, plane, plane_t, depth_m, depth_mt, ones_x, ones_yz, cover, scale)


def rows_back_kernel(*refs, weighted):
    if weighted:
        *part_refs, matrix_ref, est_ref, xz_ref, y_ref, out_ref, factor_ref = refs
    else:
        *part_refs, matrix_ref, out_ref = refs
    own_ref, *other_refs = part_refs
    planes, _, depth = out_ref.shape
    step = pl.program_id(0)

    def rows_of(ref, slot, plane):
        return ref[slot, :, plane].reshape(ref.shape[1] * ROWS, depth)

    for pair in range(0, planes, 2):
        pieces = []
        for refs_of in ((own_ref,), other_refs):
            for slot in range(own_ref.shape[0]):
                for ref in refs_of:
                    pieces.append(
                        jnp.concatenate(
                            [rows_of(ref, slot, pair), rows_of(ref, slot, pair + 1)], axis=1
                        )
                    )
        data = jnp.concatenate(pieces, axis=0)
        done = jnp.dot(matrix_ref[...], data, preferred_element_type=F32)
        for plane, part in ((pair, done[:, :depth]), (pair + 1, done[:, depth:])):
            if weighted:
                at = pl.ds(step * planes + plane, 1)
                weight = sum(y_ref[w] * xz_ref[w, at] for w in range(y_ref.shape[0]))
                part = part + QUO_MID * weight
                factor_ref[plane] = est_ref[plane] / jnp.maximum(weight, FLOOR)
            out_ref[plane] = part.astype(out_ref.dtype)


def rows_back(parts, matrix, blocks, place, weighted=None):
    depth = parts[0].shape[-1]
    rows_out = matrix.shape[0]

    def planes_of(part):
        return pl.BlockSpec(
            part.shape[:2] + (PLANES, ROWS, depth), lambda i: (0, 0, place(i), 0, 0)
        )

    block_spec = pl.BlockSpec((PLANES, rows_out, depth), lambda i: (i, 0, 0))
    in_specs = [planes_of(part) for part in parts]
    in_specs.append(pl.BlockSpec(matrix.shape, lambda i: (0, 0)))
    shape = (blocks * PLANES, rows_out, depth)
    out_specs, out_shape, extra = block_spec, jax.ShapeDtypeStruct(shape, BF16), ()
    if weighted is not None:
        extra = weighted
        in_specs.append(block_spec)
        in_specs += [pl.BlockSpec(table.shape, lambda i: (0, 0, 0)) for table in extra[1:]]
        out_specs = [block_spec] * 2
        out_shape = [jax.ShapeDtypeStruct(shape, F32)] * 2

    return pl.pallas_call(
        functools.partial(rows_back_kernel, weighted=weighted is not None),
        grid=(blocks,),
        in_specs=in_specs,
        out_specs=out_specs,
        out_shape=out_shape,
        compiler_params=pltpu.CompilerParams(vmem_limit_bytes=VMEM_LIMIT),
        cost_estimate=pl.CostEstimate(
            flops=2 * blocks * PLANES * depth * matrix.size,
            bytes_accessed=2 * blocks * PLANES * depth * (matrix.shape[1] + 2 * rows_out),
            transcendentals=0,
        ),
    )(*parts, matrix, *extra)


def on_device(estimate, raw_tiles, psf_taps, view_offsets, depth_range):
    block, half_rows, depth = estimate.shape
    slots = raw_tiles.shape[0]
    views, _, taps = psf_taps.shape
    half = taps // 2
    halo = half + MAXOFF
    tiles = lax.axis_size("tile")
    place = lax.axis_index("view")
    rows_all = half_rows * lax.axis_size("view")
    swap = [(0, 1), (1, 0)]
    up = [(i, i + 1) for i in range(tiles - 1)]
    down = [(i + 1, i) for i in range(tiles - 1)]
    quo_rows = half_rows + ROWS
    groups = quo_rows // ROWS
    est_extra = 2 * ROWS
    window = block + taps - 1

    start = (1 - place) * (half_rows - est_extra)
    edge = lax.dynamic_slice_in_dim(estimate, start, est_extra, 1)
    edge = lax.ppermute((edge - EST_MID).astype(BF16), "view", swap)
    centred = (estimate - EST_MID).astype(BF16)
    inner_est = jnp.concatenate([centred, edge], axis=1)

    other_start = (1 - place) * (half_rows - ROWS)
    cuts = [0, groups - groups // 4, groups]
    arrived = []
    for low, high in zip(cuts, cuts[1:]):
        if low > 0:
            other_start, edge = lax.optimization_barrier((other_start, edge))
        piece = lax.dynamic_slice_in_dim(
            raw_tiles, other_start + low * ROWS, (high - low) * ROWS, 2
        )
        arrived.append(lax.ppermute(piece, "view", swap))

    kernels = psf_taps / jnp.sum(psf_taps, axis=2, keepdims=True)
    rounded = lax.reduce_precision(kernels, 8, 7)
    scale = 1.0 / jnp.prod(jnp.sum(rounded, axis=2), axis=1)
    position = jnp.stack([place, lax.axis_index("tile")]).astype(jnp.int32)

    position, inner_est = lax.optimization_barrier((position, inner_est))
    below = lax.ppermute(depth_range, "tile", up)
    above = lax.ppermute(depth_range, "tile", down)

    outer_est = jnp.concatenate(
        [
            lax.ppermute(inner_est[block - halo :], "tile", up),
            lax.ppermute(inner_est[:halo], "tile", down),
        ],
        axis=0,
    )

    smem = pl.BlockSpec(memory_space=pltpu.SMEM)
    vmem = pl.BlockSpec(memory_space=pltpu.VMEM)
    shapes = [
        ((views * quo_rows, half_rows + est_extra), BF16),
        ((half_rows, views * quo_rows), BF16),
        ((views, block * SUB, window * SUB), BF16),
        ((views, window * SUB, block * SUB), BF16),
        ((views, depth, depth), BF16),
        ((views, depth, depth), BF16),
        ((views, block, SUB, depth), F32),
        ((views, quo_rows, depth), F32),
        ((views, SUB, depth), F32),
        ((views, SUB, depth), F32),
    ]
    rows_m, rows_mt, *tables = pl.pallas_call(
        functools.partial(tables_kernel, slots=slots, tiles=tiles, rows_all=rows_all),
        in_specs=[smem] * 6,
        out_specs=[vmem] * len(shapes),
        out_shape=[jax.ShapeDtypeStruct(*shape) for shape in shapes],
        compiler_params=pltpu.CompilerParams(vmem_limit_bytes=VMEM_LIMIT),
        cost_estimate=pl.CostEstimate(flops=0, bytes_accessed=30_000_000, transcendentals=0),
    )(kernels, rounded, scale, view_offsets, depth_range, position)

    table_xz, table_y = pl.pallas_call(
        functools.partial(weight_tables_kernel, rows_all=rows_all),
        in_specs=[smem] * 6,
        out_specs=[vmem] * 2,
        out_shape=[
            jax.ShapeDtypeStruct((views, block, depth), F32),
            jax.ShapeDtypeStruct((views, half_rows, depth), F32),
        ],
        compiler_params=pltpu.CompilerParams(vmem_limit_bytes=VMEM_LIMIT),
        cost_estimate=pl.CostEstimate(flops=0, bytes_accessed=8_000_000, transcendentals=0),
    )(kernels, view_offsets, below, depth_range, above, position)

    inner = rows_forward(inner_est, rows_m, views)
    outer = rows_forward(outer_est, rows_m, views)
    own_first = lax.rem(place * slots + jnp.arange(views), views)
    starts = view_offsets[own_first, 0] + (halo - half)
    base = place * ((half_rows - ROWS) // ROWS)
    base, table_xz, table_y = lax.optimization_barrier((base, table_xz, table_y))
    zero = jnp.zeros((), jnp.int32)
    parts = [
        view_pass(0, slots, 0, groups, base, starts[:slots], inner, outer, raw_tiles, tables)
    ]
    for low, high, piece in zip(cuts, cuts[1:], arrived):
        zero, parts[-1] = lax.optimization_barrier((zero, parts[-1]))
        parts.append(
            view_pass(
                1, slots, low, high - low, zero, starts[slots:], inner, outer, piece, tables
            )
        )

    side = halo // PLANES
    middle = block // PLANES
    edges = rows_back(
        parts, rows_mt, 2 * side, lambda i: jnp.where(i < side, i, i + middle)
    )
    low = lax.ppermute(edges[halo:], "tile", up)
    high = lax.ppermute(edges[:halo], "tile", down)
    kept, factor = rows_back(
        parts, rows_mt, middle, lambda i: i + side, (estimate, table_xz, table_y)
    )
    step = 2
    sides = halo // step
    whole = pl.BlockSpec((step, half_rows, depth), lambda i: (i, 0, 0))
    return pl.pallas_call(
        functools.partial(finish_kernel, sides=sides),
        grid=(block // step,),
        in_specs=[
            whole,
            whole,
            pl.BlockSpec(whole.block_shape, lambda i: (jnp.minimum(i, sides - 1), 0, 0)),
            pl.BlockSpec(whole.block_shape, lambda i: (jnp.maximum(i - sides, 0), 0, 0)),
        ],
        out_specs=whole,
        out_shape=jax.ShapeDtypeStruct(estimate.shape, F32),
        compiler_params=pltpu.CompilerParams(vmem_limit_bytes=VMEM_LIMIT),
    )(kept, factor, low, high)


def solution(mesh):
    return jax.shard_map(
        on_device,
        mesh=mesh,
        in_specs=(
            P("tile", "view", None),
            P("view", "tile", None, None),
            P(),
            P(),
            P(None, "tile", None),
        ),
        out_specs=P("tile", "view", None),
        check_vma=False,
    )
```

```python
import functools

import jax
import jax.numpy as jnp
from jax import lax
from jax.experimental import pallas as pl
from jax.experimental.pallas import tpu as pltpu
from jax.sharding import PartitionSpec as P

MAXOFF = 4
BACKGROUND = 0.1
FLOOR = 0.5
EST_MID = 1.25
QUO_MID = 1.1875
SUB = 8
ROWS = 16
PLANES = 4
F32 = jnp.float32
BF16 = jnp.bfloat16
VMEM_LIMIT = 48 * 1024 * 1024


def banded(taps, number):
    number = number.astype(F32).astype(BF16)
    total = jnp.zeros(number.shape, BF16)
    for index, tap in enumerate(taps):
        value = jnp.full(number.shape, tap, F32).astype(BF16)
        total = jnp.where(number == jnp.array(index, BF16), value, total)
    return total


def inside_sum(taps, first, step, low, high):
    total = jnp.zeros(first.shape, F32)
    for index, tap in enumerate(taps):
        at = first + step * index
        total = total + jnp.where((at >= low) & (at < high), tap, 0.0)
    return total


def tables_kernel(
    exact_ref,
    rounded_ref,
    scale_in_ref,
    offset_ref,
    range_ref,
    position_ref,
    rows_ref,
    rows_t_ref,
    plane_ref,
    plane_t_ref,
    depth_ref,
    depth_t_ref,
    ones_x_ref,
    ones_yz_ref,
    cover_ref,
    scale_ref,
    *,
    slots,
    tiles,
    rows_all,
):
    views, _, taps = exact_ref.shape
    half = taps // 2
    half_rows = rows_t_ref.shape[0]
    quo_rows = ones_yz_ref.shape[1]
    est_rows = rows_ref.shape[1]
    est_extra = est_rows - half_rows
    block, depth = ones_x_ref.shape[1], ones_x_ref.shape[3]
    place, tile = position_ref[0], position_ref[1]
    quo_first = place * (half_rows - ROWS)
    order = [lax.rem(place * slots + w, views) for w in range(views)]
    rounded = [
        [[rounded_ref[w, d, a] for a in range(taps)] for d in range(3)] for w in order
    ]
    exact = [[[exact_ref[w, d, a] for a in range(taps)] for d in range(3)] for w in order]
    offsets = [[offset_ref[w, d] for d in range(3)] for w in order]

    def iota(shape, dim):
        return lax.broadcasted_iota(jnp.int32, shape, dim)

    for w in range(views):
        ox, oy, oz = offsets[w]

        def plane_rows(i, carry, w=w):
            shape = (ROWS, plane_ref.shape[2])
            row, column = iota(shape, 0) + i * ROWS, iota(shape, 1)
            step = jnp.where(
                (row & (SUB - 1)) == (column & (SUB - 1)), (column >> 3) - (row >> 3), -1
            )
            at = pl.ds(pl.multiple_of(i * ROWS, ROWS), ROWS)
            plane_ref[w, at] = banded(rounded[w][0], step).astype(BF16)
            return carry

        lax.fori_loop(0, plane_ref.shape[1] // ROWS, plane_rows, 0)

        def plane_t_rows(i, carry, w=w):
            shape = (ROWS, plane_t_ref.shape[2])
            row, column = iota(shape, 0) + i * ROWS, iota(shape, 1)
            step = jnp.where(
                (row & (SUB - 1)) == (column & (SUB - 1)), (row >> 3) - (column >> 3), -1
            )
            at = pl.ds(pl.multiple_of(i * ROWS, ROWS), ROWS)
            plane_t_ref[w, at] = banded(rounded[w][0], step).astype(BF16)
            return carry

        lax.fori_loop(0, plane_t_ref.shape[1] // ROWS, plane_t_rows, 0)

        def depth_rows(i, carry, w=w, oz=oz):
            shape = (ROWS, depth)
            away = iota(shape, 0) + i * ROWS - iota(shape, 1)
            at = pl.ds(pl.multiple_of(i * ROWS, ROWS), ROWS)
            depth_ref[w, at] = banded(rounded[w][2], away - oz + half).astype(BF16)
            depth_t_ref[w, at] = banded(rounded[w][2], half - oz - away).astype(BF16)
            return carry

        lax.fori_loop(0, depth // ROWS, depth_rows, 0)

        def forward_rows(i, carry, w=w, oy=oy):
            shape = (ROWS, est_rows)
            position = iota(shape, 1)
            from_row = jnp.where(
                position < half_rows,
                place * half_rows + position,
                (1 - place) * half_rows
                + place * (half_rows - est_extra)
                + position
                - half_rows,
            )
            to_row = quo_first + i * ROWS + iota(shape, 0)
            value = banded(rounded[w][1], from_row - to_row - oy + half).astype(BF16)
            at = pl.multiple_of(w * quo_rows + i * ROWS, ROWS)
            rows_ref[pl.ds(at, ROWS)] = value
            return carry

        lax.fori_loop(0, quo_rows // ROWS, forward_rows, 0)

        shape = (block, SUB, depth)
        first = tile * block + iota(shape, 0) + ox - half
        ones_x_ref[w] = inside_sum(exact[w][0], first, 1, 0, tiles * block)
        first = quo_first + iota((quo_rows, depth), 0) + oy - half
        ones_y = inside_sum(exact[w][1], first, 1, 0, rows_all)
        shape = (SUB, depth)
        z = iota(shape, 1)
        ones_z = inside_sum(exact[w][2], z + oz - half, 1, 0, depth)
        ones_yz_ref[w] = EST_MID * ones_y * ones_z[:1]
        low, high = range_ref[order[w], 0, 0], range_ref[order[w], 0, 1]
        cover_ref[w] = jnp.where((z >= low) & (z < high), 1.0, 0.0)
        scale_ref[w] = jnp.full(shape, scale_in_ref[order[w]], F32)

    def back_rows(i, carry):
        shape = (ROWS, quo_rows)
        away = place * half_rows + i * ROWS + iota(shape, 0) - quo_first - iota(shape, 1)
        value = [banded(rounded[w][1], away - offsets[w][1] + half) for w in range(views)]
        at = pl.ds(pl.multiple_of(i * ROWS, ROWS), ROWS)
        rows_t_ref[at] = jnp.concatenate(value, axis=1).astype(BF16)
        return carry

    lax.fori_loop(0, half_rows // ROWS, back_rows, 0)


def weight_tables_kernel(
    exact_ref, offset_ref, below_ref, range_ref, above_ref, position_ref, xz_ref, y_ref, *, rows_all
):
    views, _, taps = exact_ref.shape
    half = taps // 2
    block, depth = xz_ref.shape[1:]
    half_rows = y_ref.shape[1]
    place = position_ref[0]

    def iota(shape, dim):
        return lax.broadcasted_iota(jnp.int32, shape, dim)

    for w in range(views):
        ox, oy, oz = (offset_ref[w, d] for d in range(3))
        exact = [[exact_ref[w, d, a] for a in range(taps)] for d in range(3)]
        plane = iota((block, depth), 0) - ox + half
        z = iota((SUB, depth), 1) - oz + half
        total = jnp.zeros((block, depth), F32)
        for side, limit in enumerate((below_ref, range_ref, above_ref)):
            low = (side - 1) * block
            share = inside_sum(exact[0], plane, -1, low, low + block)
            taken = inside_sum(exact[2], z, -1, limit[w, 0, 0], limit[w, 0, 1])
            total = total + share * taken[:1]
        xz_ref[w] = total
        first = place * half_rows + iota((half_rows, depth), 0) - oy + half
        y_ref[w] = inside_sum(exact[1], first, -1, 0, rows_all)


def rows_forward_kernel(est_ref, matrix_ref, out_ref):
    views, groups, planes, _, depth = out_ref.shape
    rows = groups * ROWS
    for pair in range(0, planes, 2):
        data = jnp.concatenate([est_ref[pair], est_ref[pair + 1]], axis=1)
        done = jnp.dot(matrix_ref[...], data, preferred_element_type=F32).astype(BF16)
        for view in range(views):
            part = done[view * rows : (view + 1) * rows]
            out_ref[view, :, pair] = part[:, :depth].reshape(groups, ROWS, depth)
            out_ref[view, :, pair + 1] = part[:, depth:].reshape(groups, ROWS, depth)


def rows_forward(est, matrix, views):
    count, rows_in, depth = est.shape
    rows = matrix.shape[0] // views
    groups = rows // ROWS
    return pl.pallas_call(
        rows_forward_kernel,
        grid=(count // PLANES,),
        in_specs=[
            pl.BlockSpec((PLANES, rows_in, depth), lambda i: (i, 0, 0)),
            pl.BlockSpec(matrix.shape, lambda i: (0, 0)),
        ],
        out_specs=pl.BlockSpec(
            (views, groups, PLANES, ROWS, depth), lambda i: (0, 0, i, 0, 0)
        ),
        out_shape=jax.ShapeDtypeStruct((views, groups, count, ROWS, depth), BF16),
        compiler_params=pltpu.CompilerParams(vmem_limit_bytes=VMEM_LIMIT),
        cost_estimate=pl.CostEstimate(
            flops=2 * count * depth * rows_in * views * rows,
            bytes_accessed=2 * (est.size + views * count * rows * depth),
            transcendentals=0,
        ),
    )(est, matrix)


def view_kernel(
    scalar_ref,
    inner_ref,
    outer_ref,
    raw_ref,
    plane_ref,
    plane_t_ref,
    depth_ref,
    depth_t_ref,
    ones_x_ref,
    ones_yz_ref,
    cover_ref,
    scale_ref,
    out_ref,
    ext_ref,
):
    slots, block, _, depth = raw_ref.shape
    halo = outer_ref.shape[1] // 2
    window = plane_ref.shape[2] // SUB
    size = block * SUB
    every = range(slots)
    starts = [scalar_ref[1 + w] for w in every]
    ext_ref[:, :halo] = outer_ref[:, :halo]
    ext_ref[:, halo : halo + block] = inner_ref[...]
    ext_ref[:, halo + block :] = outer_ref[:, halo:]
    stacked = []
    for w in every:
        source = ext_ref[w, pl.ds(starts[w], window)].astype(F32)
        halves = [
            source[:, lo : lo + SUB].reshape(window * SUB, depth) for lo in range(0, ROWS, SUB)
        ]
        data = jnp.concatenate(halves, axis=1).astype(BF16)
        planes = jnp.dot(plane_ref[w], data, preferred_element_type=F32)
        stacked.append(
            jnp.concatenate([planes[:, :depth], planes[:, depth:]], axis=0).astype(BF16)
        )
    blurred = [
        jnp.dot(stacked[w], depth_ref[w], preferred_element_type=F32).reshape(
            2, block, SUB, depth
        )
        for w in every
    ]
    quotient = []
    for w in every:
        raw = raw_ref[w].astype(F32)
        scale = scale_ref[w]
        cover = cover_ref[w] * scale
        halves = []
        for half in range(2):
            ones_yz = ones_yz_ref[w, half * SUB : (half + 1) * SUB]
            predicted = blurred[w][half] * scale + ones_x_ref[w] * ones_yz
            ratio = raw[:, half * SUB : (half + 1) * SUB] / (predicted + BACKGROUND)
            halves.append((cover * (ratio - QUO_MID)).reshape(size, depth))
        quotient.append(jnp.concatenate(halves, axis=0).astype(BF16))
    back = [
        jnp.dot(quotient[w], depth_t_ref[w], preferred_element_type=F32) for w in every
    ]
    out_ref[...] = jnp.zeros_like(out_ref)
    for w in every:
        wide = jnp.concatenate([back[w][:size], back[w][size:]], axis=1).astype(BF16)
        spread = jnp.dot(plane_t_ref[w], wide, preferred_element_type=F32)
        spread = [
            spread[:, lo : lo + depth].reshape(window, SUB, depth) for lo in (0, depth)
        ]
        out_ref[w, pl.ds(starts[w], window)] = jnp.concatenate(spread, axis=1).astype(
            out_ref.dtype
        )


def view_pass(pair, slots, first, groups, base, starts, inner, outer, raw, tables):
    _, _, block, _, depth = inner.shape
    halo2 = outer.shape[2]
    plane, plane_t, depth_m, depth_mt, ones_x, ones_yz, cover, scale = tables
    scalars = jnp.concatenate([base[None], starts]).astype(jnp.int32)

    def table(array):
        zeros = (0,) * (array.ndim - 1)
        return pl.BlockSpec((slots,) + array.shape[1:], lambda g, s: (pair,) + zeros)

    def grouped(planes):
        return pl.BlockSpec(
            (slots, None, planes, ROWS, depth), lambda g, s: (pair, first + g, 0, 0, 0)
        )

    return pl.pallas_call(
        view_kernel,
        grid_spec=pltpu.PrefetchScalarGridSpec(
            num_scalar_prefetch=1,
            grid=(groups,),
            in_specs=[
                grouped(block),
                grouped(halo2),
                pl.BlockSpec((slots, block, ROWS, depth), lambda g, s: (0, 0, s[0] + g, 0)),
                table(plane),
                table(plane_t),
                table(depth_m),
                table(depth_mt),
                table(ones_x),
                pl.BlockSpec((slots, ROWS, depth), lambda g, s: (pair, first + g, 0)),
                table(cover),
                table(scale),
            ],
            out_specs=pl.BlockSpec(
                (slots, None, block + halo2, ROWS, depth), lambda g, s: (0, g, 0, 0, 0)
            ),
            scratch_shapes=[pltpu.VMEM((slots, block + halo2, ROWS, depth), BF16)],
        ),
        out_shape=jax.ShapeDtypeStruct((slots, groups, block + halo2, ROWS, depth), BF16),
        compiler_params=pltpu.CompilerParams(vmem_limit_bytes=VMEM_LIMIT),
        cost_estimate=pl.CostEstimate(
            flops=2 * slots * groups * 3_000 * 256 * 256,
            bytes_accessed=2 * slots * groups * ROWS * depth * (5 * block),
            transcendentals=slots * block * groups * ROWS * depth,
        ),
    )(scalars, inner, outer, raw, plane, plane_t, depth_m, depth_mt, ones_x, ones_yz, cover, scale)


def rows_back_kernel(*refs):
    *part_refs, matrix_ref, out_ref = refs
    own_ref, *other_refs = part_refs
    planes, _, depth = out_ref.shape

    def rows_of(ref, slot, plane):
        return ref[slot, :, plane].reshape(ref.shape[1] * ROWS, depth)

    for pair in range(0, planes, 2):
        pieces = []
        for refs_of in ((own_ref,), other_refs):
            for slot in range(own_ref.shape[0]):
                for ref in refs_of:
                    pieces.append(
                        jnp.concatenate(
                            [rows_of(ref, slot, pair), rows_of(ref, slot, pair + 1)], axis=1
                        )
                    )
        data = jnp.concatenate(pieces, axis=0)
        done = jnp.dot(matrix_ref[...], data, preferred_element_type=F32)
        done = done.astype(out_ref.dtype)
        out_ref[pair] = done[:, :depth]
        out_ref[pair + 1] = done[:, depth:]


def rows_back(parts, matrix, blocks, place, dtype):
    depth = parts[0].shape[-1]
    rows_out = matrix.shape[0]

    def planes_of(part):
        return pl.BlockSpec(
            part.shape[:2] + (PLANES, ROWS, depth), lambda i: (0, 0, place(i), 0, 0)
        )

    block_spec = pl.BlockSpec((PLANES, rows_out, depth), lambda i: (i, 0, 0))
    in_specs = [planes_of(part) for part in parts]
    in_specs.append(pl.BlockSpec(matrix.shape, lambda i: (0, 0)))
    shape = (blocks * PLANES, rows_out, depth)
    return pl.pallas_call(
        rows_back_kernel,
        grid=(blocks,),
        in_specs=in_specs,
        out_specs=block_spec,
        out_shape=jax.ShapeDtypeStruct(shape, dtype),
        compiler_params=pltpu.CompilerParams(vmem_limit_bytes=VMEM_LIMIT),
        cost_estimate=pl.CostEstimate(
            flops=2 * blocks * PLANES * depth * matrix.size,
            bytes_accessed=2 * blocks * PLANES * depth * (matrix.shape[1] + 2 * rows_out),
            transcendentals=0,
        ),
    )(*parts, matrix)


def on_device(estimate, raw_tiles, psf_taps, view_offsets, depth_range):
    block, half_rows, depth = estimate.shape
    slots = raw_tiles.shape[0]
    views, _, taps = psf_taps.shape
    half = taps // 2
    halo = half + MAXOFF
    tiles = lax.axis_size("tile")
    place = lax.axis_index("view")
    rows_all = half_rows * lax.axis_size("view")
    swap = [(0, 1), (1, 0)]
    up = [(i, i + 1) for i in range(tiles - 1)]
    down = [(i + 1, i) for i in range(tiles - 1)]
    quo_rows = half_rows + ROWS
    groups = quo_rows // ROWS
    est_extra = 2 * ROWS
    window = block + taps - 1

    start = (1 - place) * (half_rows - est_extra)
    edge = lax.dynamic_slice_in_dim(estimate, start, est_extra, 1)
    edge = lax.ppermute((edge - EST_MID).astype(BF16), "view", swap)
    centred = (estimate - EST_MID).astype(BF16)
    inner_est = jnp.concatenate([centred, edge], axis=1)

    other_start = (1 - place) * (half_rows - ROWS)
    cuts = [0, groups - groups // 4, groups]
    arrived = []
    for low, high in zip(cuts, cuts[1:]):
        if low > 0:
            other_start, edge = lax.optimization_barrier((other_start, edge))
        piece = lax.dynamic_slice_in_dim(
            raw_tiles, other_start + low * ROWS, (high - low) * ROWS, 2
        )
        arrived.append(lax.ppermute(piece, "view", swap))

    kernels = psf_taps / jnp.sum(psf_taps, axis=2, keepdims=True)
    rounded = lax.reduce_precision(kernels, 8, 7)
    scale = 1.0 / jnp.prod(jnp.sum(rounded, axis=2), axis=1)
    position = jnp.stack([place, lax.axis_index("tile")]).astype(jnp.int32)

    position, inner_est = lax.optimization_barrier((position, inner_est))
    limits = depth_range.reshape(views * 2, 1).astype(BF16)
    limits = jnp.pad(limits, ((0, inner_est.shape[1] - views * 2), (0, 0)))
    limits = jnp.broadcast_to(limits[None], (1,) + inner_est.shape[1:])

    def with_limits(planes):
        return jnp.concatenate([planes, limits], axis=0)

    from_below = lax.ppermute(with_limits(inner_est[block - halo :]), "tile", up)
    from_above = lax.ppermute(with_limits(inner_est[:halo]), "tile", down)
    outer_est = jnp.concatenate([from_below[:halo], from_above[:halo]], axis=0)
    below, above = (
        part[halo, : views * 2, 0].reshape(views, 1, 2).astype(jnp.int32)
        for part in (from_below, from_above)
    )

    smem = pl.BlockSpec(memory_space=pltpu.SMEM)
    vmem = pl.BlockSpec(memory_space=pltpu.VMEM)
    shapes = [
        ((views * quo_rows, half_rows + est_extra), BF16),
        ((half_rows, views * quo_rows), BF16),
        ((views, block * SUB, window * SUB), BF16),
        ((views, window * SUB, block * SUB), BF16),
        ((views, depth, depth), BF16),
        ((views, depth, depth), BF16),
        ((views, block, SUB, depth), F32),
        ((views, quo_rows, depth), F32),
        ((views, SUB, depth), F32),
        ((views, SUB, depth), F32),
    ]
    rows_m, rows_mt, *tables = pl.pallas_call(
        functools.partial(tables_kernel, slots=slots, tiles=tiles, rows_all=rows_all),
        in_specs=[smem] * 6,
        out_specs=[vmem] * len(shapes),
        out_shape=[jax.ShapeDtypeStruct(*shape) for shape in shapes],
        compiler_params=pltpu.CompilerParams(vmem_limit_bytes=VMEM_LIMIT),
        cost_estimate=pl.CostEstimate(flops=0, bytes_accessed=30_000_000, transcendentals=0),
    )(kernels, rounded, scale, view_offsets, depth_range, position)

    table_xz, table_y = pl.pallas_call(
        functools.partial(weight_tables_kernel, rows_all=rows_all),
        in_specs=[smem] * 6,
        out_specs=[vmem] * 2,
        out_shape=[
            jax.ShapeDtypeStruct((views, block, depth), F32),
            jax.ShapeDtypeStruct((views, half_rows, depth), F32),
        ],
        compiler_params=pltpu.CompilerParams(vmem_limit_bytes=VMEM_LIMIT),
        cost_estimate=pl.CostEstimate(flops=0, bytes_accessed=8_000_000, transcendentals=0),
    )(kernels, view_offsets, below, depth_range, above, position)

    inner = rows_forward(inner_est, rows_m, views)
    outer = rows_forward(outer_est, rows_m, views)
    own_first = lax.rem(place * slots + jnp.arange(views), views)
    starts = view_offsets[own_first, 0] + (halo - half)
    base = place * ((half_rows - ROWS) // ROWS)
    base, table_xz, table_y = lax.optimization_barrier((base, table_xz, table_y))
    zero = jnp.zeros((), jnp.int32)
    parts = [
        view_pass(0, slots, 0, groups, base, starts[:slots], inner, outer, raw_tiles, tables)
    ]
    for low, high, piece in zip(cuts, cuts[1:], arrived):
        zero, parts[-1] = lax.optimization_barrier((zero, parts[-1]))
        parts.append(
            view_pass(
                1, slots, low, high - low, zero, starts[slots:], inner, outer, piece, tables
            )
        )

    side = halo // PLANES
    middle = block // PLANES
    edges = rows_back(
        parts, rows_mt, 2 * side, lambda i: jnp.where(i < side, i, i + middle), BF16
    )
    low = lax.ppermute(edges[halo:], "tile", up)
    high = lax.ppermute(edges[:halo], "tile", down)
    kept = rows_back(parts, rows_mt, middle, lambda i: i + side, F32)
    low = jnp.pad(low, ((0, block - halo), (0, 0), (0, 0))).astype(F32)
    high = jnp.pad(high, ((block - halo, 0), (0, 0), (0, 0))).astype(F32)
    weight = sum(
        table_xz[view][:, None, :] * table_y[view][None, :, :1] for view in range(views)
    )
    correction = kept + low + high + QUO_MID * weight
    return estimate * correction / jnp.maximum(weight, FLOOR)


def solution(mesh):
    return jax.shard_map(
        on_device,
        mesh=mesh,
        in_specs=(
            P("tile", "view", None),
            P("view", "tile", None, None),
            P(),
            P(),
            P(None, "tile", None),
        ),
        out_specs=P("tile", "view", None),
        check_vma=False,
    )
```
